32 devices in a mesh: fsdp: 8 (over y, x, core), sp: 4 (over z).
Axes of the slice: x: 2, y: 2, z: 4, core: 2. Of those that a mesh axis runs over, the one named last changes fastest.
Arguments:
- tokens: bfloat16 [16, 1024, 2560], P('fsdp', 'sp'), may hold values from -6 to 6
- segments: int32 [16, 1024], P('fsdp'), may hold values from 0 to 24, as said below
- w_query: float32 [2560, 2560], P('fsdp'), may hold values from -0.125 to 0.125
- w_key: float32 [2560, 640], P('fsdp'), may hold values from -0.125 to 0.125
- w_value: float32 [2560, 640], P('fsdp'), may hold values from -0.125 to 0.125
- w_out: float32 [2560, 2560], P('fsdp'), may hold values from -0.3125 to 0.3125
- w_gate: float32 [2560, 7168], P('fsdp'), may hold values from -0.125 to 0.125
- w_up: float32 [2560, 7168], P('fsdp'), may hold values from -0.125 to 0.125
- w_down: float32 [7168, 2560], P('fsdp'), may hold values from -0.0625 to 0.0625
- gain_attn: float32 [2560], P('fsdp'), may hold values from 0.5 to 1.5
- gain_mlp: float32 [2560], P('fsdp'), may hold values from 0.5 to 1.5
- cotangent: bfloat16 [16, 1024, 2560], P('fsdp', 'sp'), may hold values from -6 to 6
Outputs:
- layer_out: bfloat16 [16, 1024, 2560], P('fsdp', 'sp')
- grad_tokens: float32 [16, 1024, 2560], P('fsdp', 'sp')
- grad_w_query: float32 [2560, 2560], P('fsdp')
- grad_w_key: float32 [2560, 640], P('fsdp')
- grad_w_value: float32 [2560, 640], P('fsdp')
- grad_w_out: float32 [2560, 2560], P('fsdp')
- grad_w_gate: float32 [2560, 7168], P('fsdp')
- grad_w_up: float32 [2560, 7168], P('fsdp')
- grad_w_down: float32 [7168, 2560], P('fsdp')
- grad_gain_attn: float32 [2560], P('fsdp')
- grad_gain_mlp: float32 [2560], P('fsdp')
The draws below stay inside these ranges and needn't reach their ends.
Inputs may be any that keep to these rules, and one draw needn't show every extreme that they name: `segments`: in every sequence the segment ids start at 0, never fall from one position to the next, and rise by at most one; equal ids mark one document.
All inputs are finite; a program needn't handle non-finite values.
Results may differ from the reference program's by a relative error of at most 0.015.
Values may be sent and summed in bfloat16 or wider, within the bound.
No kernel may reach another device: no remote copies, remote signals or barrier semaphores. Data moves between devices by JAX's collectives and lax.ppermute only.
A program may use at most 704 MiB of HBM per device.

```python
import math
import jax
import jax.numpy as jnp
from jax import lax

D = 2560
HEADS = 32
KV_HEADS = 8
HEAD_DIM = 80
FF = 7168
SEQ_LEN = 1024
SEQS = 2
SEQUENCES = 16


def draw_segments(key, part):
    keys = jax.random.split(key, 5)
    places = jnp.arange(SEQ_LEN, dtype=jnp.int32)
    coarse_count = (SEQ_LEN + 15) // 16
    shifts = jax.random.randint(keys[0], (SEQUENCES, coarse_count), 0, 11)
    shift_here = shifts[:, places // 16]
    raw = jax.random.randint(keys[1], (SEQUENCES, SEQ_LEN), 0, 1 << 20)
    scores = jnp.right_shift(raw, shift_here) * SEQ_LEN + places[None, :]
    scores = jnp.where(places[None, :] == 0, -1, scores)
    picked_scores, cuts = lax_top(scores)
    rises = jnp.sum((places[None, :, None] == cuts[:, None, :]).astype(jnp.int32), axis=2)
    packed = jnp.cumsum(rises, axis=1)
    edge = max(2, SEQ_LEN // 16)
    opening = jax.random.randint(keys[2], (SEQUENCES, 1), 1, edge)
    closing = jax.random.randint(keys[4], (SEQUENCES, 1), SEQ_LEN - edge + 1, SEQ_LEN + 1)
    inside = (places[None, :] > opening) & (places[None, :] < closing)
    forced = (places[None, :] == opening) | (places[None, :] == closing)
    span_rises = jnp.where(forced, 1, jnp.where(inside, 0, rises))
    spanning = jnp.minimum(jnp.cumsum(span_rises, axis=1), 24)
    picked = jax.random.randint(keys[3], (SEQUENCES // SEQS, 1), 0, SEQS)
    within = jnp.broadcast_to(jnp.arange(SEQS, dtype=jnp.int32)[None, :], (SEQUENCES // SEQS, SEQS))
    chosen = (within == picked).reshape(SEQUENCES, 1)
    return jnp.where(chosen, spanning, packed).astype(jnp.int32)


def lax_top(scores):
    return jax.lax.top_k(scores, 24)


def level_of(own_key, shape, pieces, smallest, top_value):
    level, own = 1.0, jax.random.fold_in(own_key, 6)
    for position, blocks in pieces:
        draws = jnp.exp(jax.random.uniform(jax.random.fold_in(own, position), (blocks,), jnp.float32, smallest / len(pieces), top_value / len(pieces)))
        level = level * jnp.repeat(draws, shape[position] // blocks).reshape([-1 if axis == position else 1 for axis in range(len(shape))])
    return level


def noise(stream_key, extent, width, reach, cuts=(), kind=jnp.bfloat16):
    values = width * jax.random.normal(stream_key, extent, jnp.float32)
    if cuts:
        values = values * level_of(stream_key, extent, cuts, -0.22, 0.18)
    return jnp.clip(values, -reach, reach).astype(kind)


def setup_inputs(seed: int = 0) -> dict:
    splits = jax.random.split(jax.random.key(seed), 13)
    return {
        "tokens": noise(splits[0], (SEQUENCES, SEQ_LEN, D), 1.0, 6.0, ((0, 8), (1, 4))),
        "segments": draw_segments(jax.random.fold_in(splits[12], 71), 0),
        "w_query": noise(splits[2], (D, HEADS * HEAD_DIM), D ** -0.5, 0.125, ((0, 8),), jnp.float32),
        "w_key": noise(splits[3], (D, KV_HEADS * HEAD_DIM), D ** -0.5, 0.125, ((0, 8),), jnp.float32),
        "w_value": noise(splits[4], (D, KV_HEADS * HEAD_DIM), D ** -0.5, 0.125, ((0, 8),), jnp.float32),
        "w_out": noise(splits[5], (HEADS * HEAD_DIM, D), (HEADS * HEAD_DIM // 8) ** -0.5, 0.3125, ((0, 8),), jnp.float32),
        "w_gate": noise(splits[6], (D, FF), D ** -0.5, 0.125, ((0, 8),), jnp.float32),
        "w_up": noise(splits[7], (D, FF), D ** -0.5, 0.125, ((0, 8),), jnp.float32),
        "w_down": noise(splits[8], (FF, D), FF ** -0.5, 0.0625, ((0, 8),), jnp.float32),
        "gain_attn": jnp.clip(1.0 + 0.1 * jax.random.normal(splits[9], (D,), jnp.float32), 0.5, 1.5),
        "gain_mlp": jnp.clip(1.0 + 0.1 * jax.random.normal(splits[10], (D,), jnp.float32), 0.5, 1.5),
        "cotangent": noise(splits[11], (SEQUENCES, SEQ_LEN, D), 1.0, 6.0, ((0, 8), (1, 4))),
    }


epsilon = 1e-05
rope_base = 1000000.0

@jax.custom_vjp
def low(v):
    return lax.optimization_barrier(v.astype(jnp.bfloat16)).astype(jnp.float32)

@jax.custom_vjp
def low_back(v):
    return v

def low_keep(v):
    return (low(v), None)

def low_pass(kept, grad):
    return (grad,)

def back_keep(v):
    return (v, None)

def back_low(kept, grad):
    return (low(grad),)
low.defvjp(low_keep, low_pass)
low_back.defvjp(back_keep, back_low)

def matmul(left, right):
    return jnp.dot(left, right, preferred_element_type=jnp.float32, precision=lax.Precision.HIGHEST)

def rms_norm(values, gain):
    return values * lax.rsqrt(lax.optimization_barrier(jnp.mean(values * values, axis=-1, keepdims=True)) + epsilon) * gain

def rotary(field):
    half = HEAD_DIM // 2
    freqs = jnp.power(jnp.float32(rope_base), -jnp.arange(half, dtype=jnp.float32) * (2.0 / HEAD_DIM))
    angle = jnp.arange(SEQ_LEN, dtype=jnp.float32)[:, None] * freqs[None, :]
    cosine = jnp.cos(angle)[:, None, :]
    sine = jnp.sin(angle)[:, None, :]
    leading = field[..., :half]
    trailing = field[..., half:]
    return jnp.concatenate([leading * cosine - trailing * sine, trailing * cosine + leading * sine], axis=-1)

def attend(packed):
    query, keys, values, segment = packed
    group = HEADS // KV_HEADS
    scale = 1.0 / math.sqrt(HEAD_DIM)
    grouped = query.reshape(SEQ_LEN, KV_HEADS, group, HEAD_DIM)
    scores = low_back(jnp.einsum('qkgd,skd->kgqs', grouped, keys, precision=lax.Precision.HIGHEST) * scale)
    places = jnp.arange(SEQ_LEN)
    allowed = (segment[:, None] == segment[None, :]) & (places[:, None] >= places[None, :])
    scores = jnp.where(allowed, scores, -1e+30)
    topmost = lax.optimization_barrier(jnp.max(scores, axis=-1, keepdims=True))
    expo = jnp.exp(scores - topmost)
    probs = expo / lax.optimization_barrier(jnp.sum(expo, axis=-1, keepdims=True))
    output = jnp.einsum('kgqs,skd->qkgd', low(probs), values, precision=lax.Precision.HIGHEST)
    return output.reshape(SEQ_LEN, HEADS * HEAD_DIM)

def layer(inputs, segment, w_query, w_key, w_value, w_out, w_gate, w_up, w_down, gain_attn, gain_mlp):
    bundle = inputs.shape[0]
    normed_one = low(rms_norm(inputs, low(gain_attn)))
    query_lin = low_back(matmul(normed_one, low(w_query)))
    key_lin = low_back(matmul(normed_one, low(w_key)))
    query = low_back(low(rotary(query_lin.reshape(bundle, SEQ_LEN, HEADS, HEAD_DIM))))
    keys = low_back(low(rotary(key_lin.reshape(bundle, SEQ_LEN, KV_HEADS, HEAD_DIM))))
    values = low_back(low(matmul(normed_one, low(w_value)).reshape(bundle, SEQ_LEN, KV_HEADS, HEAD_DIM)))
    output = lax.map(jax.checkpoint(attend), (query, keys, values, segment))
    attn = low_back(low(output))
    resid = inputs + low_back(matmul(attn, low(w_out)))
    normed_two = low(rms_norm(resid, low(gain_mlp)))
    gate = low_back(matmul(normed_two, low(w_gate)))
    upper = low_back(matmul(normed_two, low(w_up)))
    hidden = low(jax.nn.silu(gate) * upper)
    return resid + low_back(matmul(hidden, low(w_down)))

def reference(tokens, segments, w_query, w_key, w_value, w_out, w_gate, w_up, w_down, gain_attn, gain_mlp, cotangent):
    bundle = math.gcd(SEQUENCES, max(1, 4096 // SEQ_LEN))
    rounds = SEQUENCES // bundle
    inputs = tokens.astype(jnp.float32).reshape(rounds, bundle, SEQ_LEN, D)
    segment_all = segments.reshape(rounds, bundle, SEQ_LEN)
    grads_in = cotangent.astype(jnp.float32).reshape(rounds, bundle, SEQ_LEN, D)
    weights = (w_query, w_key, w_value, w_out, w_gate, w_up, w_down, gain_attn, gain_mlp)

    def advance(totals, item):
        block_in, block_seg, block_grad = item

        def forward(values_in, *params):
            return layer(values_in, block_seg, *params)
        result, pullback = jax.vjp(forward, block_in, *weights)
        grads = pullback(block_grad)
        totals = tuple((total + grad for total, grad in zip(totals, grads[1:])))
        return (totals, (result.astype(jnp.bfloat16), grads[0]))
    zeros = tuple((jnp.zeros_like(weight) for weight in weights))
    totals, (results, grad_inputs) = lax.scan(advance, zeros, (inputs, segment_all, grads_in))
    layer_out = results.reshape(SEQUENCES, SEQ_LEN, D)
    grad_tokens = grad_inputs.reshape(SEQUENCES, SEQ_LEN, D)
    return (layer_out, grad_tokens, totals[0], totals[1], totals[2], totals[3], totals[4], totals[5], totals[6], totals[7], totals[8])
```

```python
import functools
import math

import jax
import jax.numpy as jnp
from jax import lax
from jax.experimental import pallas as pl
from jax.experimental.pallas import tpu as pltpu
from jax.sharding import PartitionSpec as P
HEADS=32; KV_HEADS=8; HEAD_DIM=80; GROUP = HEADS // KV_HEADS
SPAN = KV_HEADS * HEAD_DIM
MIB = 1 << 20
epsilon = 1e-05
rope_base = 1000000.0
LOG2E=1.4426950408889634
SCALE=1.0/math.sqrt(HEAD_DIM)
NEG=-1e30
bf=jnp.bfloat16; f32=jnp.float32
LANES=128
UNROLL=8
WIDE=KV_HEADS*LANES

def nt(a, b):
    return lax.dot_general(a, b, (((1,), (1,)), ((), ())), preferred_element_type=f32)

def tn(a, b):
    return lax.dot_general(a, b, (((0,), (0,)), ((), ())), preferred_element_type=f32)

def nn(a, b):
    return jnp.dot(a, b, preferred_element_type=f32)

def picks(n_wide, span):
    row = lax.broadcasted_iota(jnp.int32, (n_wide, span), 0)
    col = lax.broadcasted_iota(jnp.int32, (n_wide, span), 1)
    head, d = row // LANES, row % LANES
    return jnp.where((col == head * HEAD_DIM + d) & (d < HEAD_DIM), 1.0, 0.0).astype(bf)

def fwd_kernel(Z, meta, q_ref, *refs):
    kv_refs = refs[:Z]
    sq_ref, sk_ref, o_ref, lse_ref, sel, q_s, k_s, vt_s, b_s, o_s = refs[Z:]
    seq = pl.program_id(0)
    L = q_ref.shape[1]
    span = KV_HEADS * HEAD_DIM
    mine = meta[0]
    steps = mine - meta[1 + seq] + 1

    @pl.when(seq == 0)
    def _():
        sel[...] = picks(WIDE, span)

    for c in range(GROUP):
        q_s[:, WIDE*c:WIDE*(c+1)] = nt(q_ref[0, :, span*c:span*(c+1)], sel[...]).astype(bf)
    seg_q = sq_ref[0]
    tri = lax.broadcasted_iota(jnp.int32, (L, L), 1) >= lax.broadcasted_iota(jnp.int32, (L, L), 0)
    ones_row = lax.broadcasted_iota(jnp.int32, (WIDE, L), 0) % LANES == HEAD_DIM
    for k in range(Z):
        @pl.when(k < steps)
        def _():
            k_s[k] = nt(kv_refs[k][0, :, :span], sel[...]).astype(bf)
            vt_s[k] = jnp.where(ones_row, 1.0, nt(sel[...], kv_refs[k][0, :, span:])).astype(bf)
            seg_k = sk_ref[0, pl.ds(pl.multiple_of((mine - k) * L, L), L), :]
            ok = seg_q == seg_k
            b_s[k] = jnp.where(ok & tri if k == 0 else ok, 0.0, NEG)
    def unit(u, _):
        hs = [u * UNROLL + i for i in range(UNROLL)]
        lanes = [pl.ds(pl.multiple_of((h // GROUP) * LANES, LANES), LANES) for h in hs]
        wides = [pl.ds(pl.multiple_of(h * LANES, LANES), LANES) for h in hs]
        def block(k, carry):
            bias = b_s[k]
            out = []
            for i in range(UNROLL):
                s = nt(k_s[k, :, lanes[i]], q_s[:, wides[i]]) + bias
                m = jnp.max(s, axis=0, keepdims=True)
                if carry is not None:
                    m = jnp.maximum(carry[i][0], m)
                p = jnp.exp2((s - m) * (SCALE * LOG2E)).astype(bf)
                o = nn(vt_s[k, lanes[i], :], p)
                if carry is not None:
                    o = carry[i][1] * jnp.exp2((carry[i][0] - m) * (SCALE * LOG2E)) + o
                out.append((m, o))
            return tuple(out)
        done = lax.fori_loop(1, steps, block, block(0, None))
        for i in range(UNROLL):
            m, acc = done[i]
            total = acc[HEAD_DIM:HEAD_DIM+1, :]
            o_s[wides[i], :] = (acc * (1.0 / total)).astype(bf)
            lse_ref[0, pl.ds(hs[i], 1), :] = m * (SCALE * LOG2E) + jnp.log2(total)
        return 0
    lax.fori_loop(0, HEADS // UNROLL, unit, 0)
    for c in range(GROUP):
        o_ref[0, :, span*c:span*(c+1)] = tn(o_s[WIDE*c:WIDE*(c+1), :], sel[...]).astype(bf)

def attend(meta, q, kvs, seg_q, seg_k):
    B, L, W = q.shape; Z = len(kvs); S = Z * L
    span = KV_HEADS * HEAD_DIM
    vm = pltpu.VMEM
    spec = lambda *s: pl.BlockSpec((1,) + s, lambda b, meta: (b,) + (0,) * len(s))
    return pl.pallas_call(
        functools.partial(fwd_kernel, Z),
        grid_spec=pltpu.PrefetchScalarGridSpec(
            num_scalar_prefetch=1, grid=(B,),
            in_specs=[spec(L, W)] + [spec(L, 2 * span)] * Z + [spec(1, L), spec(S, 1)],
            out_specs=[spec(L, W), spec(HEADS, L)],
            scratch_shapes=[vm((WIDE, span), bf), vm((L, HEADS * LANES), bf), vm((Z, L, WIDE), bf), vm((Z, WIDE, L), bf),
                            vm((Z, L, L), f32), vm((HEADS * LANES, L), bf)]),
        out_shape=[jax.ShapeDtypeStruct((B, L, W), bf), jax.ShapeDtypeStruct((B, HEADS, L), f32)],
        compiler_params=pltpu.CompilerParams(vmem_limit_bytes=56 << 20),
        name="attend_fwd",
    )(meta, q, *kvs, seg_q, seg_k)

def turn(x, cos, left, right):
    n = x.shape[1]
    return x * cos + pltpu.roll(x, n - HEAD_DIM // 2, 1) * left + pltpu.roll(x, HEAD_DIM // 2, 1) * right

def bwd_kernel(Z, meta, q_ref, *refs):
    kv_refs = refs[:Z]
    o_ref, do_ref, lse_ref, sq_ref, sk_ref, cq_ref, lq_ref, rq_ref, ck_ref, lk_ref, rk_ref = refs[Z:Z+11]
    dq_ref = refs[Z+11]; dkv_refs = refs[Z+12:2*Z+12]
    sel, q_s, d_s, k_s, kt_s, v_s, b_s, dqt_s, dk_s, dv_s, delta_s = refs[2*Z+12:]
    seq = pl.program_id(0)
    L = q_ref.shape[1]
    span = KV_HEADS * HEAD_DIM
    mine = meta[0]
    steps = mine - meta[1 + seq] + 1

    @pl.when(seq == 0)
    def _():
        sel[...] = picks(WIDE, span)

    head_row = lax.broadcasted_iota(jnp.int32, (KV_HEADS * 2, span), 0)
    column = lax.broadcasted_iota(jnp.int32, (KV_HEADS * 2, span), 1)
    heads = jnp.where(column // HEAD_DIM == head_row, 1.0, 0.0).astype(bf)
    for c in range(GROUP):
        cols = slice(span*c, span*(c+1)); wide = slice(WIDE*c, WIDE*(c+1))
        q_s[:, wide] = nt(q_ref[0, :, cols], sel[...]).astype(bf)
        d = do_ref[0, :, cols]
        d_s[:, wide] = nt(d, sel[...]).astype(bf)
        prod = o_ref[0, :, cols].astype(f32) * d.astype(f32)
        high = prod.astype(bf)
        rest = (prod - high.astype(f32)).astype(bf)
        delta_s[KV_HEADS*c:KV_HEADS*(c+1), :] = (nt(heads, high) + nt(heads, rest))[:KV_HEADS]
    seg_q = sq_ref[0]
    tri = lax.broadcasted_iota(jnp.int32, (L, L), 1) >= lax.broadcasted_iota(jnp.int32, (L, L), 0)
    for k in range(Z):
        @pl.when(k < steps)
        def _():
            k_s[k] = nt(kv_refs[k][0, :, :span], sel[...]).astype(bf)
            kt_s[k] = nt(sel[...], kv_refs[k][0, :, :span]).astype(bf)
            v_s[k] = nt(kv_refs[k][0, :, span:], sel[...]).astype(bf)
            seg_k = sk_ref[0, pl.ds(pl.multiple_of((mine - k) * L, L), L), :]
            ok = seg_q == seg_k
            b_s[k] = jnp.where(ok & tri if k == 0 else ok, 0.0, NEG)
    dqt_s[...] = jnp.zeros_like(dqt_s)
    def group(g, _):
        lanes = pl.ds(pl.multiple_of(g * LANES, LANES), LANES)
        def block(k, _):
            key = k_s[k, :, lanes]; value = v_s[k, :, lanes]; key_t = kt_s[k, lanes, :]
            bias = b_s[k]
            dk = jnp.zeros((L, LANES), f32); dv = jnp.zeros((L, LANES), f32)
            for i in range(GROUP):
                h = g * GROUP + i
                wide = pl.ds(pl.multiple_of(h * LANES, LANES), LANES)
                q = q_s[:, wide]; d = d_s[:, wide]
                p = jnp.exp2(nt(key, q) * (SCALE * LOG2E) + (bias - lse_ref[0, pl.ds(h, 1), :]))
                ds = (p * (nt(value, d) - delta_s[pl.ds(h, 1), :])).astype(bf)
                dv = dv + nn(p.astype(bf), d)
                dk = dk + nn(ds, q)
                dqt_s[wide, :] += nn(key_t, ds)
            dk_s[k, :, lanes] = (dk * SCALE).astype(bf)
            dv_s[k, :, lanes] = dv.astype(bf)
            return 0
        lax.fori_loop(0, steps, block, 0)
        return 0
    lax.fori_loop(0, KV_HEADS, group, 0)
    for c in range(GROUP):
        x = tn((dqt_s[WIDE*c:WIDE*(c+1), :] * SCALE).astype(bf), sel[...])
        dq_ref[0, :, span*c:span*(c+1)] = turn(x, cq_ref[...], lq_ref[...], rq_ref[...]).astype(bf)
    for k in range(Z):
        @pl.when(k < steps)
        def _():
            spot = pl.ds(pl.multiple_of((mine - k) * L, L), L)
            dkv_refs[k][0, :, :span] = turn(nn(dk_s[k], sel[...]), ck_ref[spot, :], lk_ref[spot, :], rk_ref[spot, :]).astype(bf)
            dkv_refs[k][0, :, span:] = nn(dv_s[k], sel[...]).astype(bf)
        @pl.when(k >= steps)
        def _():
            dkv_refs[k][...] = jnp.zeros_like(dkv_refs[k])

def attend_back(meta, q, kvs, o, do, lse, seg_q, seg_k, tab_q, tab_k):
    B, L, W = q.shape; Z = len(kvs); S = Z * L
    span = KV_HEADS * HEAD_DIM
    spec = lambda *s: pl.BlockSpec((1,) + s, lambda b, meta: (b,) + (0,) * len(s))
    fixed = lambda t: pl.BlockSpec(t.shape, lambda b, meta: (0, 0))
    vm = pltpu.VMEM
    return pl.pallas_call(
        functools.partial(bwd_kernel, Z),
        grid_spec=pltpu.PrefetchScalarGridSpec(
            num_scalar_prefetch=1, grid=(B,),
            in_specs=[spec(L, W)] + [spec(L, 2 * span)] * Z + [spec(L, W), spec(L, W), spec(HEADS, L), spec(1, L), spec(S, 1)]
              + [fixed(t) for t in tab_q + tab_k],
            out_specs=[spec(L, W)] + [spec(L, 2 * span)] * Z,
            scratch_shapes=[vm((WIDE, span), bf), vm((L, HEADS * LANES), bf), vm((L, HEADS * LANES), bf), vm((Z, L, WIDE), bf), vm((Z, WIDE, L), bf),
                            vm((Z, L, WIDE), bf), vm((Z, L, L), f32), vm((HEADS * LANES, L), f32), vm((Z, L, WIDE), bf), vm((Z, L, WIDE), bf), vm((HEADS, L), f32)]),
        out_shape=[jax.ShapeDtypeStruct((B, L, W), bf)] + [jax.ShapeDtypeStruct((B, L, 2 * span), bf)] * Z,
        compiler_params=pltpu.CompilerParams(vmem_limit_bytes=60 << 20),
        name="attend_bwd",
    )(meta, q, *kvs, o, do, lse, seg_q, seg_k, *tab_q, *tab_k)


def proj_kernel(turned, x_ref, w_ref, c_ref, l_ref, r_ref, y_ref):
    y = jnp.dot(x_ref[...], w_ref[...], preferred_element_type=f32)
    column = pl.program_id(0)

    @pl.when(column < turned)
    def _():
        y_ref[...] = turn(y, c_ref[...], l_ref[...], r_ref[...]).astype(bf)

    @pl.when(column >= turned)
    def _():
        y_ref[...] = y.astype(bf)


def project(x, w, tables, columns, turned):
    rows, width = x.shape
    length = tables[0].shape[0]
    return pl.pallas_call(
        functools.partial(proj_kernel, turned),
        grid=(columns, rows // length),
        in_specs=[
            pl.BlockSpec((length, width), lambda c, b: (b, 0)),
            pl.BlockSpec((width, SPAN), lambda c, b: (0, c)),
        ]
        + [pl.BlockSpec((length, SPAN), lambda c, b: (0, 0))] * 3,
        out_specs=pl.BlockSpec((length, SPAN), lambda c, b: (b, c)),
        out_shape=jax.ShapeDtypeStruct((rows, columns * SPAN), bf),
        compiler_params=pltpu.CompilerParams(vmem_limit_bytes=40 * MIB),
        cost_estimate=pl.CostEstimate(
            flops=2 * rows * width * columns * SPAN,
            bytes_accessed=2 * width * (rows + columns * SPAN),
            transcendentals=0,
        ),
        name="project",
    )(x, w, *tables)


def contract_last(left, right):
    return lax.dot_general(left, right, (((1,), (1,)), ((), ())), preferred_element_type=f32)


def contract_first(left, right):
    return lax.dot_general(left, right, (((0,), (0,)), ((), ())), preferred_element_type=f32)


def norm_back(grad_normed, unit, rstd, gain):
    scaled = grad_normed * gain
    return rstd * (scaled - unit * jnp.mean(scaled * unit, axis=-1, keepdims=True))


def gather(x, axis_name):
    return lax.all_gather(x, axis_name, axis=0, tiled=True)


def scatter(x, axis_name):
    return lax.psum_scatter(x, axis_name, scatter_dimension=0, tiled=True)


def right(x, count, axis_name="sp"):
    return lax.ppermute(x, axis_name, [(i, i + 1) for i in range(count)])


def left(x, count, parts, axis_name="sp"):
    return lax.ppermute(x, axis_name, [(i, i - 1) for i in range(parts - count, parts)])


def add(a, b):
    return a if b is None else (a.astype(f32) + b.astype(f32)).astype(bf)


def after(x, *others):
    others = [t for t in others if t is not None]
    return lax.optimization_barrier((x, *others))[0] if others else x


class Sum:
    def __init__(self, x, axis, parts, here):
        self.part = lambda c: lax.dynamic_index_in_dim(x, lax.rem(c + parts, parts), axis, keepdims=False)
        self.parts, self.here, self.step, self.up, self.down = parts, here, 1, None, None

    def go(self, *gates):
        if self.step >= self.parts:
            return ()
        up, down = self.up, self.down
        if up is not None:
            up, down = after(up, *gates), after(down, *gates)
        up = add(self.part(self.here + self.parts - self.step), up)
        down = add(self.part(self.here - self.parts + self.step), down)
        self.up, self.down = right(up, self.step), left(down, self.step, self.parts)
        self.step += 1
        return up, down

    def end(self, *gates):
        while self.step < self.parts:
            self.go()
        up, down = after(self.up, *gates), after(self.down, *gates)
        return (self.part(self.here).astype(f32) + up.astype(f32) + down.astype(f32)).astype(bf)


class Spread:
    def __init__(self, x, axis, parts, here, dtype, outs=1):
        self.x, self.axis, self.parts, self.here, self.dtype = x, axis, parts, here, dtype
        self.ups, self.downs = [x], [x]
        self.outs = outs

    def rise(self, *gates):
        step = len(self.ups)
        if step >= self.parts:
            return None
        send = after(self.ups[-1], *gates)
        self.ups.append(lax.ppermute(send, "sp", [(i, i + 1) for i in range(step - 1, self.parts - 1)]))
        return self.ups[-1]

    def fall(self, *gates):
        step = len(self.downs)
        if step >= self.parts:
            return None
        send = after(self.downs[-1], *gates)
        self.downs.append(lax.ppermute(send, "sp", [(i, i - 1) for i in range(1, self.parts - step + 1)]))
        return self.downs[-1]

    def go(self, *gates):
        self.rise(*gates)
        self.fall(*gates)

    def end(self):
        for _ in range(self.parts):
            self.go()
        pieces = [(self.here, self.x)]
        for step in range(1, self.parts):
            index = lax.rem(self.here - step + self.parts, self.parts)
            pieces.append((index, self.ups[step] + self.downs[self.parts - step]))
        whole = []
        for out in range(self.outs):
            choose = (lambda t: t) if self.outs == 1 else (lambda t: t[out])
            shape = choose(self.x).shape
            total = jnp.zeros(shape[: self.axis] + (self.parts,) + shape[self.axis :], self.dtype)
            for index, value in pieces:
                total = lax.dynamic_update_index_in_dim(total, choose(value).astype(self.dtype), index, self.axis)
            whole.append(total)
        return whole[0] if self.outs == 1 else whole


def split(x, parts):
    return x.reshape((parts, x.shape[0] // parts) + x.shape[1:])


def across(x, parts, here):
    shard = Sum(split(x, parts), 0, parts, here).end()
    return Spread(shard, 0, parts, here, f32).end().reshape(x.shape)


def tables_of(positions):
    half = HEAD_DIM // 2
    freqs = jnp.power(f32(rope_base), -jnp.arange(half, dtype=f32) * (2.0 / HEAD_DIM))
    angle = positions[:, None] * freqs[None, :]
    cosine, sine = jnp.cos(angle), jnp.sin(angle)
    none = jnp.zeros_like(sine)
    wide = lambda a, b: jnp.tile(jnp.concatenate([a, b], axis=1), (1, KV_HEADS))
    return wide(cosine, cosine), wide(sine, none), wide(none, sine)


def local(
    tokens, segments, w_query, w_key, w_value, w_out, w_gate, w_up, w_down, gain_attn, gain_mlp, cotangent
):
    seqs, length, width = tokens.shape
    seq_len = segments.shape[1]
    parts = lax.axis_size("sp")
    owners = lax.axis_size("fsdp")
    here = lax.axis_index("sp")
    rows = seqs * length
    ff = w_gate.shape[1]
    cols = ff // owners
    share = w_gate.shape[0] // parts

    own = lambda w: lax.dynamic_slice_in_dim(w, here * share, share, 0).astype(bf)
    pair = jnp.stack([own(w_gate), own(w_up)], axis=0).reshape(2 * share, ff)
    pair = lax.all_to_all(pair, "fsdp", split_axis=1, concat_axis=0, tiled=True)
    pair = pair.reshape(owners, 2, share, cols).transpose(0, 2, 1, 3).reshape(owners, share, 2 * cols)
    gains = jnp.pad(jnp.stack([gain_attn, gain_mlp], axis=1), ((0, 0), (0, 126)))
    kv_full = gather(jnp.concatenate([w_key.astype(bf), w_value.astype(bf), gains.astype(bf)], axis=1), "fsdp")
    gain_one = kv_full[:, 2 * SPAN].astype(f32)
    gain_two = kv_full[:, 2 * SPAN + 1].astype(f32)
    down = w_down.astype(bf)
    cot = cotangent.reshape(rows, width)

    cosine, sine_low, sine_high = tables_of(jnp.arange(seq_len, dtype=f32))
    mine = lambda t: lax.dynamic_slice_in_dim(t, here * length, length, 0)
    tab_own = (mine(cosine), mine(sine_low), mine(sine_high))
    tab_q = [tab_own[0], tab_own[1], -tab_own[2]]
    tab_k = [cosine, sine_low, -sine_high]
    tab_fwd = (tab_own[0], -tab_own[1], tab_own[2])

    seg_own = lax.dynamic_slice_in_dim(segments, here * length, length, 1)
    ends = segments.reshape(seqs, parts, length)[:, :, -1]
    first = jnp.sum((ends < seg_own[:, :1]).astype(jnp.int32), axis=1)
    meta = jnp.concatenate([here.astype(jnp.int32)[None], first])

    inputs = tokens.reshape(rows, width).astype(f32)
    rstd_one = lax.rsqrt(jnp.mean(inputs * inputs, axis=-1, keepdims=True) + epsilon)
    unit_one = inputs * rstd_one
    normed_one = after((unit_one * gain_one).astype(bf), pair)
    kv_own = project(normed_one, kv_full, tab_fwd, 2, 1).reshape(seqs, length, 2 * SPAN)
    query_full = gather(after(w_query.astype(bf), kv_own), "fsdp")
    kvs = [kv_own]
    for step in range(1, parts):
        kvs.append(lax.ppermute(kvs[-1], "sp", [(i, i + 1) for i in range(step - 1, parts - 1)]))
    query = project(normed_one, query_full, tab_fwd, HEADS // KV_HEADS, HEADS // KV_HEADS)
    ring = Spread(pair, 1, parts, here, bf)
    fallen = ring.fall()
    out_full = gather(after(w_out.astype(bf), query, kvs[-1], fallen), "fsdp")
    query = query.reshape(seqs, length, HEADS * HEAD_DIM)
    risen = ring.rise(kvs[-1])
    attn, logsum = attend(
        meta, query, kvs, seg_own[:, None, :], segments[:, :, None]
    )
    ring.fall()
    attn = after(attn, risen, ring.downs[-1])
    ring.rise(attn)
    attn_flat = attn.reshape(rows, HEADS * HEAD_DIM)
    resid = inputs + jnp.dot(attn_flat, out_full, preferred_element_type=f32)
    rstd_two = lax.rsqrt(jnp.mean(resid * resid, axis=-1, keepdims=True) + epsilon)
    unit_two = resid * rstd_two
    normed_two = (unit_two * gain_two).astype(bf)
    normed_all = gather(normed_two, "fsdp")
    cot_all = gather(after(cot, normed_two), "fsdp")
    ring.rise(normed_two)
    pair = ring.end().reshape(width, 2 * cols)

    both = jnp.dot(normed_all, pair, preferred_element_type=f32)
    grad_hidden = contract_last(cot_all, down)
    gate_pre, up_pre = both[:, :cols], both[:, cols:]
    sigma = jax.nn.sigmoid(gate_pre)
    silu_value = gate_pre * sigma
    hidden = (silu_value * up_pre).astype(bf)
    grad_gate = (grad_hidden * up_pre * sigma * (1.0 + gate_pre * (1.0 - sigma))).astype(bf)
    grad_up = (grad_hidden * silu_value).astype(bf)
    joined = lambda a, b: jnp.concatenate([a, b], axis=1)
    term_down = contract_first(hidden, cot_all).astype(bf)
    ring_down = Sum(split(term_down, parts), 0, parts, here)
    ring_down.go()
    grad_gate, grad_up = after(grad_gate, term_down), after(grad_up, term_down)
    grad_normed_two = contract_last(joined(grad_gate, grad_up), pair).astype(bf)
    sent = ring_down.go()
    grad_gate = after(grad_gate, grad_normed_two, *sent)
    grad_normed_two = scatter(after(grad_normed_two, *sent), "fsdp")
    rows_of = lambda t: t.reshape(owners, parts, share, cols)
    term_gate = contract_first(normed_all, grad_gate).astype(bf)
    ring_gate = Sum(rows_of(term_gate), 1, parts, here)
    grad_up = after(grad_up, *ring_gate.go(), *ring_down.go(term_gate))
    term_up = contract_first(normed_all, grad_up).astype(bf)
    ring_up = Sum(rows_of(term_up), 1, parts, here)
    hidden = after(hidden, *ring_up.go(), *ring_gate.go(term_up))
    grad_down = Spread(ring_down.end(), 0, parts, here, f32)
    grad_down.go()
    mlp_out = jnp.dot(after(hidden, grad_down.x), down, preferred_element_type=f32).astype(bf)
    sent = ring_gate.go() + ring_up.go()
    mlp_out = after(mlp_out, *sent)
    grad_down.go(mlp_out)
    shard_gate = ring_gate.end(mlp_out)
    grad_normed_two = after(grad_normed_two, mlp_out, shard_gate, *ring_up.go(mlp_out)).astype(f32)
    mlp_out = scatter(mlp_out, "fsdp")

    grad_resid = cot.astype(f32) + norm_back(grad_normed_two, unit_two, rstd_two, gain_two)
    grad_branch = grad_resid.astype(bf)
    grad_attn = contract_last(grad_branch, out_full).astype(bf)
    term_out = contract_first(attn_flat, after(grad_branch, grad_attn)).astype(bf)
    shard_pair = jnp.stack([shard_gate, ring_up.end()], axis=1)
    shard_pair = lax.all_to_all(shard_pair, "fsdp", split_axis=0, concat_axis=0, tiled=True)
    shard_pair = shard_pair.transpose(1, 2, 0, 3).reshape(2, share, ff)
    shard_out = scatter(after(term_out, shard_pair), "fsdp")
    grad_pair = Spread(shard_pair, 0, parts, here, f32, outs=2)
    grad_pair.go()
    grad_down.go(term_out)
    grad_attn = after(grad_attn, term_out, shard_pair).reshape(seqs, length, HEADS * HEAD_DIM)
    grad_query, passing = [], []
    for b in range(seqs):
        one = lambda t: t[b : b + 1]
        grad_q, *grad_kvs = attend_back(
            jnp.stack([meta[0], meta[1 + b]]), one(query), [one(t) for t in kvs], one(attn), one(grad_attn), one(logsum),
            seg_own[b : b + 1, None, :], segments[b : b + 1, :, None], tab_q, tab_k
        )
        grad_query.append(grad_q)
        passing.append([grad_kvs, None])
        gates = (grad_q,)
        if b < seqs - 1:
            grad_pair.go(*gates)
            grad_attn = after(grad_attn, grad_q, grad_pair.ups[1], grad_pair.downs[1])
    for step in range(1, parts):
        for b in range(seqs):
            grad_kvs, held = passing[b]
            passing[b][1] = left(add(grad_kvs[parts - step], held), step, parts)
        if step == 1:
            grad_query = jnp.concatenate(grad_query, axis=0).reshape(rows, HEADS * HEAD_DIM)
            term_query = contract_first(normed_one, grad_query).astype(bf)
            grad_pair.go(term_query)
            for held in passing:
                held[1] = after(held[1], term_query)
    shard_query = scatter(term_query, "fsdp")
    layer_out = (resid + after(mlp_out, term_query).astype(f32)).astype(bf)
    grad_kv = jnp.concatenate([add(grad_kvs[0], held) for grad_kvs, held in passing], axis=0)
    grad_kv = grad_kv.reshape(rows, 2 * SPAN)
    shard_kv = scatter(contract_first(normed_one, grad_kv).astype(bf), "fsdp")
    grad_normed_one = contract_last(grad_query, query_full) + contract_last(grad_kv, kv_full[:, : 2 * SPAN])
    grad_inputs = grad_resid + norm_back(grad_normed_one, unit_one, rstd_one, gain_one)
    grad_w_gate, grad_w_up = (t.reshape(parts * share, ff) for t in grad_pair.end())
    grad_down = grad_down.end().reshape(w_down.shape)
    shard_both = across(joined(shard_out, shard_query), parts, here)
    shard_out, shard_query = shard_both[:, :width], shard_both[:, width:]
    shard_kv = lax.psum(shard_kv, "sp").astype(f32)
    grad_key, grad_value = shard_kv[:, :SPAN], shard_kv[:, SPAN:]
    along = lambda w, g: jnp.sum(w.astype(bf).astype(f32) * g, axis=1)
    low_gain = lambda gain: gain.astype(bf).astype(f32)
    grad_gain_attn = along(w_query, shard_query) + along(w_key, grad_key) + along(w_value, grad_value)
    grad_gain_mlp = along(w_gate, grad_w_gate) + along(w_up, grad_w_up)
    return (
        layer_out.reshape(seqs, length, width),
        grad_inputs.reshape(seqs, length, width),
        shard_query,
        grad_key,
        grad_value,
        shard_out,
        grad_w_gate,
        grad_w_up,
        grad_down,
        grad_gain_attn / low_gain(gain_attn),
        grad_gain_mlp / low_gain(gain_mlp),
    )


def solution(mesh):
    data, rows, lone = P("fsdp", "sp", None), P("fsdp", None), P("fsdp")
    return jax.shard_map(
        local,
        mesh=mesh,
        in_specs=(data, rows) + (rows,) * 7 + (lone, lone, data),
        out_specs=(data, data) + (rows,) * 7 + (lone, lone),
        check_vma=False,
    )
```

```python
import functools
import math

import jax
import jax.numpy as jnp
from jax import lax
from jax.experimental import pallas as pl
from jax.experimental.pallas import tpu as pltpu
from jax.sharding import PartitionSpec as P
HEADS=32; KV_HEADS=8; HEAD_DIM=80; GROUP = HEADS // KV_HEADS
SPAN = KV_HEADS * HEAD_DIM
MIB = 1 << 20
epsilon = 1e-05
rope_base = 1000000.0
LOG2E=1.4426950408889634
SCALE=1.0/math.sqrt(HEAD_DIM)
NEG=-1e30
bf=jnp.bfloat16; f32=jnp.float32
LANES=128
UNROLL=8
WIDE=KV_HEADS*LANES

def nt(a, b):
    return lax.dot_general(a, b, (((1,), (1,)), ((), ())), preferred_element_type=f32)

def tn(a, b):
    return lax.dot_general(a, b, (((0,), (0,)), ((), ())), preferred_element_type=f32)

def nn(a, b):
    return jnp.dot(a, b, preferred_element_type=f32)

def picks(n_wide, span):
    row = lax.broadcasted_iota(jnp.int32, (n_wide, span), 0)
    col = lax.broadcasted_iota(jnp.int32, (n_wide, span), 1)
    head, d = row // LANES, row % LANES
    return jnp.where((col == head * HEAD_DIM + d) & (d < HEAD_DIM), 1.0, 0.0).astype(bf)

def fwd_kernel(Z, meta, q_ref, *refs):
    kv_refs = refs[:Z]
    sq_ref, sk_ref, o_ref, lse_ref, sel, q_s, k_s, vt_s, b_s, o_s = refs[Z:]
    seq = pl.program_id(0)
    L = q_ref.shape[1]
    span = KV_HEADS * HEAD_DIM
    mine = meta[0]
    steps = mine - meta[1 + seq] + 1

    @pl.when(seq == 0)
    def _():
        sel[...] = picks(WIDE, span)

    for c in range(GROUP):
        q_s[:, WIDE*c:WIDE*(c+1)] = nt(q_ref[0, :, span*c:span*(c+1)], sel[...]).astype(bf)
    seg_q = sq_ref[0]
    tri = lax.broadcasted_iota(jnp.int32, (L, L), 1) >= lax.broadcasted_iota(jnp.int32, (L, L), 0)
    ones_row = lax.broadcasted_iota(jnp.int32, (WIDE, L), 0) % LANES == HEAD_DIM
    for k in range(Z):
        @pl.when(k < steps)
        def _():
            k_s[k] = nt(kv_refs[k][0, :, :span], sel[...]).astype(bf)
            vt_s[k] = jnp.where(ones_row, 1.0, nt(sel[...], kv_refs[k][0, :, span:])).astype(bf)
            seg_k = sk_ref[0, pl.ds(pl.multiple_of((mine - k) * L, L), L), :]
            ok = seg_q == seg_k
            b_s[k] = jnp.where(ok & tri if k == 0 else ok, 0.0, NEG)
    def unit(u, _):
        hs = [u * UNROLL + i for i in range(UNROLL)]
        lanes = [pl.ds(pl.multiple_of((h // GROUP) * LANES, LANES), LANES) for h in hs]
        wides = [pl.ds(pl.multiple_of(h * LANES, LANES), LANES) for h in hs]
        def block(k, carry):
            bias = b_s[k]
            out = []
            for i in range(UNROLL):
                s = nt(k_s[k, :, lanes[i]], q_s[:, wides[i]]) + bias
                m = jnp.max(s, axis=0, keepdims=True)
                if carry is not None:
                    m = jnp.maximum(carry[i][0], m)
                p = jnp.exp2((s - m) * (SCALE * LOG2E)).astype(bf)
                o = nn(vt_s[k, lanes[i], :], p)
                if carry is not None:
                    o = carry[i][1] * jnp.exp2((carry[i][0] - m) * (SCALE * LOG2E)) + o
                out.append((m, o))
            return tuple(out)
        done = lax.fori_loop(1, steps, block, block(0, None))
        for i in range(UNROLL):
            m, acc = done[i]
            total = acc[HEAD_DIM:HEAD_DIM+1, :]
            o_s[wides[i], :] = (acc * (1.0 / total)).astype(bf)
            lse_ref[0, pl.ds(hs[i], 1), :] = m * (SCALE * LOG2E) + jnp.log2(total)
        return 0
    lax.fori_loop(0, HEADS // UNROLL, unit, 0)
    for c in range(GROUP):
        o_ref[0, :, span*c:span*(c+1)] = tn(o_s[WIDE*c:WIDE*(c+1), :], sel[...]).astype(bf)

def attend(meta, q, kvs, seg_q, seg_k):
    B, L, W = q.shape; Z = len(kvs); S = Z * L
    span = KV_HEADS * HEAD_DIM
    vm = pltpu.VMEM
    spec = lambda *s: pl.BlockSpec((1,) + s, lambda b, meta: (b,) + (0,) * len(s))
    return pl.pallas_call(
        functools.partial(fwd_kernel, Z),
        grid_spec=pltpu.PrefetchScalarGridSpec(
            num_scalar_prefetch=1, grid=(B,),
            in_specs=[spec(L, W)] + [spec(L, 2 * span)] * Z + [spec(1, L), spec(S, 1)],
            out_specs=[spec(L, W), spec(HEADS, L)],
            scratch_shapes=[vm((WIDE, span), bf), vm((L, HEADS * LANES), bf), vm((Z, L, WIDE), bf), vm((Z, WIDE, L), bf),
                            vm((Z, L, L), f32), vm((HEADS * LANES, L), bf)]),
        out_shape=[jax.ShapeDtypeStruct((B, L, W), bf), jax.ShapeDtypeStruct((B, HEADS, L), f32)],
        compiler_params=pltpu.CompilerParams(vmem_limit_bytes=56 << 20),
        name="attend_fwd",
    )(meta, q, *kvs, seg_q, seg_k)

def turn(x, cos, left, right):
    n = x.shape[1]
    return x * cos + pltpu.roll(x, n - HEAD_DIM // 2, 1) * left + pltpu.roll(x, HEAD_DIM // 2, 1) * right

def bwd_kernel(Z, meta, q_ref, *refs):
    kv_refs = refs[:Z]
    o_ref, do_ref, lse_ref, sq_ref, sk_ref, cq_ref, lq_ref, rq_ref, ck_ref, lk_ref, rk_ref = refs[Z:Z+11]
    dq_ref = refs[Z+11]; dkv_refs = refs[Z+12:2*Z+12]
    sel, q_s, d_s, k_s, kt_s, v_s, b_s, dqt_s, dk_s, dv_s, delta_s = refs[2*Z+12:]
    seq = pl.program_id(0)
    L = q_ref.shape[1]
    span = KV_HEADS * HEAD_DIM
    mine = meta[0]
    steps = mine - meta[1 + seq] + 1

    @pl.when(seq == 0)
    def _():
        sel[...] = picks(WIDE, span)

    head_row = lax.broadcasted_iota(jnp.int32, (KV_HEADS * 2, span), 0)
    column = lax.broadcasted_iota(jnp.int32, (KV_HEADS * 2, span), 1)
    heads = jnp.where(column // HEAD_DIM == head_row, 1.0, 0.0).astype(bf)
    for c in range(GROUP):
        cols = slice(span*c, span*(c+1)); wide = slice(WIDE*c, WIDE*(c+1))
        q_s[:, wide] = nt(q_ref[0, :, cols], sel[...]).astype(bf)
        d = do_ref[0, :, cols]
        d_s[:, wide] = nt(d, sel[...]).astype(bf)
        prod = o_ref[0, :, cols].astype(f32) * d.astype(f32)
        high = prod.astype(bf)
        rest = (prod - high.astype(f32)).astype(bf)
        delta_s[KV_HEADS*c:KV_HEADS*(c+1), :] = (nt(heads, high) + nt(heads, rest))[:KV_HEADS]
    seg_q = sq_ref[0]
    tri = lax.broadcasted_iota(jnp.int32, (L, L), 1) >= lax.broadcasted_iota(jnp.int32, (L, L), 0)
    for k in range(Z):
        @pl.when(k < steps)
        def _():
            k_s[k] = nt(kv_refs[k][0, :, :span], sel[...]).astype(bf)
            kt_s[k] = nt(sel[...], kv_refs[k][0, :, :span]).astype(bf)
            v_s[k] = nt(kv_refs[k][0, :, span:], sel[...]).astype(bf)
            seg_k = sk_ref[0, pl.ds(pl.multiple_of((mine - k) * L, L), L), :]
            ok = seg_q == seg_k
            b_s[k] = jnp.where(ok & tri if k == 0 else ok, 0.0, NEG)
    dqt_s[...] = jnp.zeros_like(dqt_s)
    def group(g, _):
        lanes = pl.ds(pl.multiple_of(g * LANES, LANES), LANES)
        def block(k, _):
            key = k_s[k, :, lanes]; value = v_s[k, :, lanes]; key_t = kt_s[k, lanes, :]
            bias = b_s[k]
            dk = jnp.zeros((L, LANES), f32); dv = jnp.zeros((L, LANES), f32)
            for i in range(GROUP):
                h = g * GROUP + i
                wide = pl.ds(pl.multiple_of(h * LANES, LANES), LANES)
                q = q_s[:, wide]; d = d_s[:, wide]
                p = jnp.exp2(nt(key, q) * (SCALE * LOG2E) + (bias - lse_ref[0, pl.ds(h, 1), :]))
                ds = (p * (nt(value, d) - delta_s[pl.ds(h, 1), :])).astype(bf)
                dv = dv + nn(p.astype(bf), d)
                dk = dk + nn(ds, q)
                dqt_s[wide, :] += nn(key_t, ds)
            dk_s[k, :, lanes] = (dk * SCALE).astype(bf)
            dv_s[k, :, lanes] = dv.astype(bf)
            return 0
        lax.fori_loop(0, steps, block, 0)
        return 0
    lax.fori_loop(0, KV_HEADS, group, 0)
    for c in range(GROUP):
        x = tn((dqt_s[WIDE*c:WIDE*(c+1), :] * SCALE).astype(bf), sel[...])
        dq_ref[0, :, span*c:span*(c+1)] = turn(x, cq_ref[...], lq_ref[...], rq_ref[...]).astype(bf)
    for k in range(Z):
        @pl.when(k < steps)
        def _():
            spot = pl.ds(pl.multiple_of((mine - k) * L, L), L)
            dkv_refs[k][0, :, :span] = turn(nn(dk_s[k], sel[...]), ck_ref[spot, :], lk_ref[spot, :], rk_ref[spot, :]).astype(bf)
            dkv_refs[k][0, :, span:] = nn(dv_s[k], sel[...]).astype(bf)
        @pl.when(k >= steps)
        def _():
            dkv_refs[k][...] = jnp.zeros_like(dkv_refs[k])

def attend_back(meta, q, kvs, o, do, lse, seg_q, seg_k, tab_q, tab_k):
    B, L, W = q.shape; Z = len(kvs); S = Z * L
    span = KV_HEADS * HEAD_DIM
    spec = lambda *s: pl.BlockSpec((1,) + s, lambda b, meta: (b,) + (0,) * len(s))
    fixed = lambda t: pl.BlockSpec(t.shape, lambda b, meta: (0, 0))
    vm = pltpu.VMEM
    return pl.pallas_call(
        functools.partial(bwd_kernel, Z),
        grid_spec=pltpu.PrefetchScalarGridSpec(
            num_scalar_prefetch=1, grid=(B,),
            in_specs=[spec(L, W)] + [spec(L, 2 * span)] * Z + [spec(L, W), spec(L, W), spec(HEADS, L), spec(1, L), spec(S, 1)]
              + [fixed(t) for t in tab_q + tab_k],
            out_specs=[spec(L, W)] + [spec(L, 2 * span)] * Z,
            scratch_shapes=[vm((WIDE, span), bf), vm((L, HEADS * LANES), bf), vm((L, HEADS * LANES), bf), vm((Z, L, WIDE), bf), vm((Z, WIDE, L), bf),
                            vm((Z, L, WIDE), bf), vm((Z, L, L), f32), vm((HEADS * LANES, L), f32), vm((Z, L, WIDE), bf), vm((Z, L, WIDE), bf), vm((HEADS, L), f32)]),
        out_shape=[jax.ShapeDtypeStruct((B, L, W), bf)] + [jax.ShapeDtypeStruct((B, L, 2 * span), bf)] * Z,
        compiler_params=pltpu.CompilerParams(vmem_limit_bytes=60 << 20),
        name="attend_bwd",
    )(meta, q, *kvs, o, do, lse, seg_q, seg_k, *tab_q, *tab_k)


def proj_kernel(turned, x_ref, w_ref, c_ref, l_ref, r_ref, y_ref):
    y = jnp.dot(x_ref[...], w_ref[...], preferred_element_type=f32)
    column = pl.program_id(0)

    @pl.when(column < turned)
    def _():
        y_ref[...] = turn(y, c_ref[...], l_ref[...], r_ref[...]).astype(bf)

    @pl.when(column >= turned)
    def _():
        y_ref[...] = y.astype(bf)


def project(x, w, tables, columns, turned):
    rows, width = x.shape
    length = tables[0].shape[0]
    return pl.pallas_call(
        functools.partial(proj_kernel, turned),
        grid=(columns, rows // length),
        in_specs=[
            pl.BlockSpec((length, width), lambda c, b: (b, 0)),
            pl.BlockSpec((width, SPAN), lambda c, b: (0, c)),
        ]
        + [pl.BlockSpec((length, SPAN), lambda c, b: (0, 0))] * 3,
        out_specs=pl.BlockSpec((length, SPAN), lambda c, b: (b, c)),
        out_shape=jax.ShapeDtypeStruct((rows, columns * SPAN), bf),
        compiler_params=pltpu.CompilerParams(vmem_limit_bytes=40 * MIB),
        cost_estimate=pl.CostEstimate(
            flops=2 * rows * width * columns * SPAN,
            bytes_accessed=2 * width * (rows + columns * SPAN),
            transcendentals=0,
        ),
        name="project",
    )(x, w, *tables)


def contract_last(left, right):
    return lax.dot_general(left, right, (((1,), (1,)), ((), ())), preferred_element_type=f32)


def contract_first(left, right):
    return lax.dot_general(left, right, (((0,), (0,)), ((), ())), preferred_element_type=f32)


def norm_back(grad_normed, unit, rstd, gain):
    scaled = grad_normed * gain
    return rstd * (scaled - unit * jnp.mean(scaled * unit, axis=-1, keepdims=True))


def gather(x, axis_name):
    return lax.all_gather(x, axis_name, axis=0, tiled=True)


def scatter(x, axis_name):
    return lax.psum_scatter(x, axis_name, scatter_dimension=0, tiled=True)


def right(x, count, axis_name="sp"):
    return lax.ppermute(x, axis_name, [(i, i + 1) for i in range(count)])


def left(x, count, parts, axis_name="sp"):
    return lax.ppermute(x, axis_name, [(i, i - 1) for i in range(parts - count, parts)])


def add(a, b):
    return a if b is None else (a.astype(f32) + b.astype(f32)).astype(bf)


def after(x, *others):
    others = [t for t in others if t is not None]
    return lax.optimization_barrier((x, *others))[0] if others else x


class Sum:
    def __init__(self, x, axis, parts, here):
        self.part = lambda c: lax.dynamic_index_in_dim(x, lax.rem(c + parts, parts), axis, keepdims=False)
        self.parts, self.here, self.step, self.up, self.down = parts, here, 1, None, None

    def go(self, *gates):
        if self.step >= self.parts:
            return ()
        up, down = self.up, self.down
        if up is not None:
            up, down = after(up, *gates), after(down, *gates)
        up = add(self.part(self.here + self.parts - self.step), up)
        down = add(self.part(self.here - self.parts + self.step), down)
        self.up, self.down = right(up, self.step), left(down, self.step, self.parts)
        self.step += 1
        return up, down

    def end(self, *gates):
        while self.step < self.parts:
            self.go()
        up, down = after(self.up, *gates), after(self.down, *gates)
        return (self.part(self.here).astype(f32) + up.astype(f32) + down.astype(f32)).astype(bf)


class Spread:
    def __init__(self, x, axis, parts, here, dtype, outs=1):
        self.x, self.axis, self.parts, self.here, self.dtype = x, axis, parts, here, dtype
        self.ups, self.downs = [x], [x]
        self.outs = outs

    def rise(self, *gates):
        step = len(self.ups)
        if step >= self.parts:
            return None
        send = after(self.ups[-1], *gates)
        self.ups.append(lax.ppermute(send, "sp", [(i, i + 1) for i in range(step - 1, self.parts - 1)]))
        return self.ups[-1]

    def fall(self, *gates):
        step = len(self.downs)
        if step >= self.parts:
            return None
        send = after(self.downs[-1], *gates)
        self.downs.append(lax.ppermute(send, "sp", [(i, i - 1) for i in range(1, self.parts - step + 1)]))
        return self.downs[-1]

    def go(self, *gates):
        self.rise(*gates)
        self.fall(*gates)

    def end(self):
        for _ in range(self.parts):
            self.go()
        pieces = [(self.here, self.x)]
        for step in range(1, self.parts):
            index = lax.rem(self.here - step + self.parts, self.parts)
            pieces.append((index, self.ups[step] + self.downs[self.parts - step]))
        whole = []
        for out in range(self.outs):
            choose = (lambda t: t) if self.outs == 1 else (lambda t: t[out])
            shape = choose(self.x).shape
            total = jnp.zeros(shape[: self.axis] + (self.parts,) + shape[self.axis :], self.dtype)
            for index, value in pieces:
                total = lax.dynamic_update_index_in_dim(total, choose(value).astype(self.dtype), index, self.axis)
            whole.append(total)
        return whole[0] if self.outs == 1 else whole


def split(x, parts):
    return x.reshape((parts, x.shape[0] // parts) + x.shape[1:])


def across(x, parts, here):
    shard = Sum(split(x, parts), 0, parts, here).end()
    return Spread(shard, 0, parts, here, f32).end().reshape(x.shape)


def tables_of(positions):
    half = HEAD_DIM // 2
    freqs = jnp.power(f32(rope_base), -jnp.arange(half, dtype=f32) * (2.0 / HEAD_DIM))
    angle = positions[:, None] * freqs[None, :]
    cosine, sine = jnp.cos(angle), jnp.sin(angle)
    none = jnp.zeros_like(sine)
    wide = lambda a, b: jnp.tile(jnp.concatenate([a, b], axis=1), (1, KV_HEADS))
    return wide(cosine, cosine), wide(sine, none), wide(none, sine)


def local(
    tokens, segments, w_query, w_key, w_value, w_out, w_gate, w_up, w_down, gain_attn, gain_mlp, cotangent
):
    seqs, length, width = tokens.shape
    seq_len = segments.shape[1]
    parts = lax.axis_size("sp")
    owners = lax.axis_size("fsdp")
    here = lax.axis_index("sp")
    rows = seqs * length
    ff = w_gate.shape[1]
    cols = ff // owners
    share = w_gate.shape[0] // parts

    own = lambda w: lax.dynamic_slice_in_dim(w, here * share, share, 0).astype(bf)
    pair = jnp.stack([own(w_gate), own(w_up)], axis=0).reshape(2 * share, ff)
    pair = lax.all_to_all(pair, "fsdp", split_axis=1, concat_axis=0, tiled=True)
    pair = pair.reshape(owners, 2, share, cols).transpose(0, 2, 1, 3).reshape(owners, share, 2 * cols)
    gains = jnp.pad(jnp.stack([gain_attn, gain_mlp], axis=1), ((0, 0), (0, 126)))
    kv_full = gather(jnp.concatenate([w_key.astype(bf), w_value.astype(bf), gains.astype(bf)], axis=1), "fsdp")
    gain_one = kv_full[:, 2 * SPAN].astype(f32)
    gain_two = kv_full[:, 2 * SPAN + 1].astype(f32)
    down = w_down.astype(bf)
    cot = cotangent.reshape(rows, width)

    cosine, sine_low, sine_high = tables_of(jnp.arange(seq_len, dtype=f32))
    mine = lambda t: lax.dynamic_slice_in_dim(t, here * length, length, 0)
    tab_own = (mine(cosine), mine(sine_low), mine(sine_high))
    tab_q = [tab_own[0], tab_own[1], -tab_own[2]]
    tab_k = [cosine, sine_low, -sine_high]
    tab_fwd = (tab_own[0], -tab_own[1], tab_own[2])

    seg_own = lax.dynamic_slice_in_dim(segments, here * length, length, 1)
    ends = segments.reshape(seqs, parts, length)[:, :, -1]
    first = jnp.sum((ends < seg_own[:, :1]).astype(jnp.int32), axis=1)
    meta = jnp.concatenate([here.astype(jnp.int32)[None], first])

    inputs = tokens.reshape(rows, width).astype(f32)
    rstd_one = lax.rsqrt(jnp.mean(inputs * inputs, axis=-1, keepdims=True) + epsilon)
    unit_one = inputs * rstd_one
    normed_one = after((unit_one * gain_one).astype(bf), pair)
    kv_own = project(normed_one, kv_full, tab_fwd, 2, 1).reshape(seqs, length, 2 * SPAN)
    query_full = gather(after(w_query.astype(bf), kv_own), "fsdp")
    kvs = [kv_own]
    for step in range(1, parts):
        kvs.append(lax.ppermute(kvs[-1], "sp", [(i, i + 1) for i in range(step - 1, parts - 1)]))
    query = project(normed_one, query_full, tab_fwd, HEADS // KV_HEADS, HEADS // KV_HEADS)
    ring = Spread(pair, 1, parts, here, bf)
    fallen = ring.fall()
    out_full = gather(after(w_out.astype(bf), query, kvs[-1], fallen), "fsdp")
    query = query.reshape(seqs, length, HEADS * HEAD_DIM)
    risen = ring.rise(kvs[-1])
    attn, logsum = attend(
        meta, query, kvs, seg_own[:, None, :], segments[:, :, None]
    )
    ring.fall()
    attn = after(attn, risen, ring.downs[-1])
    ring.rise(attn)
    attn_flat = attn.reshape(rows, HEADS * HEAD_DIM)
    resid = inputs + jnp.dot(attn_flat, out_full, preferred_element_type=f32)
    rstd_two = lax.rsqrt(jnp.mean(resid * resid, axis=-1, keepdims=True) + epsilon)
    unit_two = resid * rstd_two
    normed_two = (unit_two * gain_two).astype(bf)
    normed_all = gather(normed_two, "fsdp")
    cot_all = gather(after(cot, normed_two), "fsdp")
    ring.rise(normed_two)
    pair = ring.end().reshape(width, 2 * cols)

    both = jnp.dot(normed_all, pair, preferred_element_type=f32)
    grad_hidden = contract_last(cot_all, down)
    gate_pre, up_pre = both[:, :cols], both[:, cols:]
    sigma = jax.nn.sigmoid(gate_pre)
    silu_value = gate_pre * sigma
    hidden = (silu_value * up_pre).astype(bf)
    grad_gate = (grad_hidden * up_pre * sigma * (1.0 + gate_pre * (1.0 - sigma))).astype(bf)
    grad_up = (grad_hidden * silu_value).astype(bf)
    joined = lambda a, b: jnp.concatenate([a, b], axis=1)
    term_down = contract_first(hidden, cot_all).astype(bf)
    ring_down = Sum(split(term_down, parts), 0, parts, here)
    ring_down.go()
    grad_gate, grad_up = after(grad_gate, term_down), after(grad_up, term_down)
    grad_normed_two = contract_last(joined(grad_gate, grad_up), pair).astype(bf)
    sent = ring_down.go()
    grad_gate = after(grad_gate, grad_normed_two, *sent)
    grad_normed_two = scatter(after(grad_normed_two, *sent), "fsdp")
    rows_of = lambda t: t.reshape(owners, parts, share, cols)
    term_gate = contract_first(normed_all, grad_gate).astype(bf)
    ring_gate = Sum(rows_of(term_gate), 1, parts, here)
    grad_up = after(grad_up, *ring_gate.go(), *ring_down.go(term_gate))
    term_up = contract_first(normed_all, grad_up).astype(bf)
    ring_up = Sum(rows_of(term_up), 1, parts, here)
    hidden = after(hidden, *ring_up.go(), *ring_gate.go(term_up))
    grad_down = Spread(ring_down.end(), 0, parts, here, f32)
    grad_down.go()
    mlp_out = jnp.dot(after(hidden, grad_down.x), down, preferred_element_type=f32).astype(bf)
    sent = ring_gate.go() + ring_up.go()
    ready = after(mlp_out, *sent)
    mlp_out = scatter(mlp_out, "fsdp")
    grad_down.go(ready)
    shard_gate = ring_gate.end(ready)
    grad_normed_two = after(grad_normed_two, ready, shard_gate, *ring_up.go(ready)).astype(f32)

    grad_resid = cot.astype(f32) + norm_back(grad_normed_two, unit_two, rstd_two, gain_two)
    grad_branch = grad_resid.astype(bf)
    grad_attn = contract_last(grad_branch, out_full).astype(bf)
    term_out = contract_first(attn_flat, after(grad_branch, grad_attn)).astype(bf)
    shard_pair = jnp.stack([shard_gate, ring_up.end()], axis=1)
    shard_pair = lax.all_to_all(shard_pair, "fsdp", split_axis=0, concat_axis=0, tiled=True)
    shard_pair = shard_pair.transpose(1, 2, 0, 3).reshape(2, share, ff)
    shard_out = scatter(term_out, "fsdp")
    grad_pair = Spread(shard_pair, 0, parts, here, f32, outs=2)
    grad_pair.go()
    grad_down.go(term_out)
    grad_attn = after(grad_attn, term_out, shard_pair).reshape(seqs, length, HEADS * HEAD_DIM)
    grad_query, passing = [], []
    for b in range(seqs):
        one = lambda t: t[b : b + 1]
        grad_q, *grad_kvs = attend_back(
            jnp.stack([meta[0], meta[1 + b]]), one(query), [one(t) for t in kvs], one(attn), one(grad_attn), one(logsum),
            seg_own[b : b + 1, None, :], segments[b : b + 1, :, None], tab_q, tab_k
        )
        grad_query.append(grad_q)
        passing.append([grad_kvs, None])
        gates = (grad_q,)
        if b < seqs - 1:
            grad_pair.go(*gates)
            grad_attn = after(grad_attn, grad_q, grad_pair.ups[1], grad_pair.downs[1])
    for step in range(1, parts):
        for b in range(seqs):
            grad_kvs, held = passing[b]
            passing[b][1] = left(add(grad_kvs[parts - step], held), step, parts)
        if step == 1:
            grad_query = jnp.concatenate(grad_query, axis=0).reshape(rows, HEADS * HEAD_DIM)
            term_query = contract_first(normed_one, grad_query).astype(bf)
            grad_pair.go(term_query)
            for held in passing:
                held[1] = after(held[1], term_query)
    shard_query = scatter(term_query, "fsdp")
    layer_out = (resid + after(mlp_out, term_query).astype(f32)).astype(bf)
    grad_kv = jnp.concatenate([add(grad_kvs[0], held) for grad_kvs, held in passing], axis=0)
    grad_kv = grad_kv.reshape(rows, 2 * SPAN)
    shard_kv = scatter(contract_first(normed_one, grad_kv).astype(bf), "fsdp")
    grad_normed_one = contract_last(grad_query, query_full) + contract_last(grad_kv, kv_full[:, : 2 * SPAN])
    grad_inputs = grad_resid + norm_back(grad_normed_one, unit_one, rstd_one, gain_one)
    grad_w_gate, grad_w_up = (t.reshape(parts * share, ff) for t in grad_pair.end())
    grad_down = grad_down.end().reshape(w_down.shape)
    shard_both = across(joined(shard_out, shard_query), parts, here)
    shard_out, shard_query = shard_both[:, :width], shard_both[:, width:]
    shard_kv = lax.psum(shard_kv, "sp").astype(f32)
    grad_key, grad_value = shard_kv[:, :SPAN], shard_kv[:, SPAN:]
    along = lambda w, g: jnp.sum(w.astype(bf).astype(f32) * g, axis=1)
    low_gain = lambda gain: gain.astype(bf).astype(f32)
    grad_gain_attn = along(w_query, shard_query) + along(w_key, grad_key) + along(w_value, grad_value)
    grad_gain_mlp = along(w_gate, grad_w_gate) + along(w_up, grad_w_up)
    return (
        layer_out.reshape(seqs, length, width),
        grad_inputs.reshape(seqs, length, width),
        shard_query,
        grad_key,
        grad_value,
        shard_out,
        grad_w_gate,
        grad_w_up,
        grad_down,
        grad_gain_attn / low_gain(gain_attn),
        grad_gain_mlp / low_gain(gain_mlp),
    )


def solution(mesh):
    data, rows, lone = P("fsdp", "sp", None), P("fsdp", None), P("fsdp")
    return jax.shard_map(
        local,
        mesh=mesh,
        in_specs=(data, rows) + (rows,) * 7 + (lone, lone, data),
        out_specs=(data, data) + (rows,) * 7 + (lone, lone),
        check_vma=False,
    )
```
